32 devices in a mesh: groups: 2 (over y), pool: 4 (over z), heads: 4 (over x, core).
Axes of the slice: x: 2, y: 2, z: 4, core: 2. Of those that a mesh axis runs over, the one named last changes fastest.
Arguments:
- queries: bfloat16 [128, 6144], P(('groups', 'pool'), 'heads'), parts along dimension 0, may hold values from -40 to 40
- new_kv: bfloat16 [2, 128, 1024], P(None, ('groups', 'pool'), 'heads'), parts along dimension 1, may hold values from -6 to 6
- cache_kv: bfloat16 [2, 8192, 1024], P(None, ('groups', 'pool'), 'heads'), parts along dimension 1, may hold values from -5 to 5
- cache_len: int32 [8], P(('groups', 'pool')), parts along dimension 0, may hold values from 256 to 1024, as said below
- residual: bfloat16 [128, 6144], P(('groups', 'pool', 'heads')), parts along dimension 0, may hold values from -6 to 6
- out_weight: bfloat16 [6144, 6144], P('heads', 'pool'), may hold values from -0.078125 to 0.078125
- norm_gain: float32 [6144], replicated, may hold values from 0.25 to 1.75
- expert_ids: int32 [128, 4], P(('groups', 'pool', 'heads')), parts along dimension 0, may hold values from 0 to 7, all different within a row; in each aligned block of 4 rows (0 to 3, 4 to 7, ...) at most 3 rows name the same one
- gate_raw: float32 [128, 4], P(('groups', 'pool', 'heads')), parts along dimension 0, may hold values from 0.05 to 1
- expert_in: bfloat16 [8, 6144, 5376], P('pool', 'heads'), may hold values from -0.078125 to 0.078125
- expert_out: bfloat16 [8, 5376, 6144], P('pool', None, 'heads'), may hold values from -0.078125 to 0.078125
Outputs:
- layer_out: bfloat16 [128, 6144], P(('groups', 'pool', 'heads')), parts along dimension 0
The draws below stay inside these ranges and needn't reach their ends.
There are 2 independent parts, one for each index of `groups`. The reference program is written for one: setup_inputs(seed, part) draws one part's arguments, and reference() takes and returns one part's arrays. A program takes and returns all parts, laid end to end along the dimension named above; an argument that names none is the same for every part. Nothing has to cross between parts.
Inputs may be any that keep to these rules, and one draw needn't show every extreme that they name: `expert_ids`: each aligned block of 4 rows (the rows of one device) names no expert in more than 3 rows, and some expert reaches 3 in some block. `cache_len`: some request's cache is full in every draw.
All inputs are finite; a program needn't handle non-finite values.
Results may differ from the reference program's by a relative error of at most 0.0085.
Values may be sent and summed in bfloat16 or wider, within the bound.
A program may use at most 192 MiB of HBM per device.

```python
import math
import jax
import jax.numpy as jnp
import numpy as np
from jax import lax

D = 6144
QHEADS = 48
KVHEADS = 8
HEAD_DIM = 128
EXPERTS = 8
TOPK = 4
FW = 5376
NGRAM = 4
ROWS_DEV = 4
CACHE = 1024
CAP = 3
SLICES = 1
REPLICA_ROWS = 16
ROWS_ALL = 64
CACHE_ALL = 4096
N_POOL = 4
N_HEADS = 4


def draw_cache_kv(key, part):
    key = jax.random.fold_in(key, 1)
    return jnp.clip(jax.random.normal(key, (2, CACHE_ALL, KVHEADS * HEAD_DIM), jnp.float32), -5.0, 5.0).astype(jnp.bfloat16)


def draw_queries(key, part):
    key = jax.random.fold_in(key, 2)
    return jnp.clip(jax.random.normal(key, (ROWS_ALL, D), jnp.float32), -5.0, 5.0).astype(jnp.bfloat16)


def draw_cache_len(key, part):
    key = jax.random.fold_in(key, 3)
    first_key, second_key = jax.random.split(key)
    replicas = CACHE_ALL // CACHE
    lengths = jax.random.randint(first_key, (replicas,), max(CACHE // 4, 2), CACHE + 1)
    full_one = jax.random.randint(second_key, (), 0, replicas)
    return lengths.at[full_one].set(CACHE).astype(jnp.int32)


def block_scale(rng, extent, cuts, low, top_value):
    level, own = 1.0, jax.random.fold_in(rng, 6)
    for axis_at, parts in cuts:
        draws = jnp.exp(jax.random.uniform(jax.random.fold_in(own, axis_at), (parts,), jnp.float32, low / len(cuts), top_value / len(cuts)))
        level = level * jnp.repeat(draws, extent[axis_at] // parts).reshape([-1 if axis == axis_at else 1 for axis in range(len(extent))])
    return level


def routed_block(stream_key, own, number, rows, amount, top, reach, slope):
    order = jax.random.permutation(stream_key, amount)
    heavy_load, usual = shares(amount, rows * top, reach, slope, True), shares(amount, rows * top, reach, slope, False)
    places = jnp.arange(amount)

    def named(sizes, rotation):
        used = int((sizes > 0).sum())
        fixed = max(1, used // 4)
        moved = fixed + (places - fixed + rotation * (used - fixed)) % max(1, amount - fixed)
        return jnp.zeros((amount,), jnp.int32).at[order[jnp.where(places < fixed, places, moved)]].set(jnp.asarray(sizes, jnp.int32))

    sizes = jnp.where(number % 4 == 0, named(heavy_load, number // 4), named(usual, number - number // 4 - 1))
    mixed = jax.random.permutation(jax.random.fold_in(own, 3), amount)
    source_of, taker = mixed[0:amount // 2 * 2:2], mixed[1:amount // 2 * 2:2]
    room = jnp.minimum(sizes[source_of] - 1, reach - sizes[taker]) // 2
    room = jnp.where((source_of == order[0]) | (taker == order[0]) | (sizes[taker] == 0), 0, jnp.maximum(room, 0))
    moved = jax.random.randint(jax.random.fold_in(own, 4), (amount // 2,), 0, 1 << 20) % (room + 1)
    sizes = sizes.at[source_of].add(-moved).at[taker].add(moved)
    items = jnp.searchsorted(jnp.cumsum(sizes), jnp.arange(rows * top), side="right").astype(jnp.int32)
    listing = items.reshape(top, rows).T
    listing = listing[jax.random.permutation(jax.random.fold_in(own, 1), rows)]
    rotation = jax.random.randint(jax.random.fold_in(own, 2), (rows, 1), 0, top)
    return jnp.take_along_axis(listing, (jnp.arange(top)[None, :] + rotation) % top, axis=1)


def shares(amount, total, reach, skew, full):
    loads = [(1 << 20) // math.isqrt(grade ** skew) + 1 for grade in range(1, amount + 1)]
    largest = reach if full else min(reach, max(-(-total // amount), total * loads[0] // sum(loads)))
    least = 1 if total - largest >= amount - 1 else 0
    given, rest = [largest] + [least] * (amount - 1), total - largest - least * (amount - 1)
    while rest > 0:
        free = [i for i in range(1, amount) if given[i] < largest] or [i for i in range(1, amount) if given[i] < reach]
        mass, budget = sum([loads[i] for i in free]), rest
        for i in free:
            more = min(reach - given[i], max(1, budget * loads[i] // mass), rest)
            given[i] = given[i] + more
            rest = rest - more
    return np.array(given)


def noise(rng, shape, scale, most, cuts=(), kind=jnp.bfloat16):
    array = scale * jax.random.normal(rng, shape, jnp.float32)
    if cuts:
        array = array * block_scale(rng, shape, cuts, -0.22, 0.18)
    return jnp.clip(array, -most, most).astype(kind)


def setup_inputs(seed: int = 0, part: int = 0) -> dict:
    arg_keys = jax.random.split(jax.random.key(seed), 12)
    part_keys = jax.random.split(jax.random.fold_in(arg_keys[11], part), 12)
    queries = draw_queries(jax.random.fold_in(jax.random.fold_in(arg_keys[11], part), 71), part)
    new_kv = noise(part_keys[1], (2, ROWS_ALL, KVHEADS * HEAD_DIM), 1.0, 6.0, ((1, 4), (2, 4)))
    cache_kv = draw_cache_kv(jax.random.fold_in(jax.random.fold_in(arg_keys[11], part), 71), part)
    cache_len = draw_cache_len(jax.random.fold_in(jax.random.fold_in(arg_keys[11], part), 71), part)
    residual = noise(part_keys[4], (ROWS_ALL, D), 1.0, 6.0, ((0, 16),))
    out_weight = noise(arg_keys[5], (D, D), D ** -0.5, 0.078125, ((0, 4), (1, 4)))
    norm_gain = jnp.clip(1.0 + 0.15 * jax.random.normal(arg_keys[6], (D,), jnp.float32), 0.25, 1.75)
    expert_ids_keys = jax.random.split(jax.random.fold_in(part_keys[7], 1), ROWS_ALL // ROWS_DEV)
    expert_ids_turns = jax.random.permutation(jax.random.fold_in(part_keys[7], 3), ROWS_ALL // ROWS_DEV)
    expert_ids = jax.vmap(lambda own, number: routed_block(jax.random.fold_in(part_keys[7], 2), own, number, ROWS_DEV, EXPERTS, TOPK, CAP, 2))(expert_ids_keys, expert_ids_turns).reshape((ROWS_ALL, TOPK))
    gate_raw = jnp.clip(jnp.exp(math.log(1.0) - 2.9957323 * jax.random.uniform(part_keys[8], (ROWS_ALL, TOPK), jnp.float32) ** block_scale(part_keys[8], (ROWS_ALL, TOPK), ((0, 16),), -0.2, 0.2)), 0.05, 1.0)
    expert_in = noise(arg_keys[9], (EXPERTS * SLICES, D, FW // SLICES), D ** -0.5, 0.078125, ((0, 4), (1, 4)))
    expert_out = noise(arg_keys[10], (EXPERTS * SLICES, FW // SLICES, D), FW ** -0.5, 0.078125, ((0, 4), (2, 4)))
    return {"queries": queries, "new_kv": new_kv, "cache_kv": cache_kv, "cache_len": cache_len, "residual": residual, "out_weight": out_weight, "norm_gain": norm_gain, "expert_ids": expert_ids, "gate_raw": gate_raw, "expert_in": expert_in, "expert_out": expert_out}


def attend(queries_one, keys_cache, vals_cache, keys_window, vals_window, length):
    group = QHEADS // KVHEADS
    local_q = queries_one.astype(jnp.float32).reshape(REPLICA_ROWS, KVHEADS, group, HEAD_DIM)
    cache_keys = keys_cache.astype(jnp.float32).reshape(CACHE, KVHEADS, HEAD_DIM)
    cache_vals = vals_cache.astype(jnp.float32).reshape(CACHE, KVHEADS, HEAD_DIM)
    window_keys = keys_window.astype(jnp.float32).reshape(REPLICA_ROWS, KVHEADS, HEAD_DIM)
    window_vals = vals_window.astype(jnp.float32).reshape(REPLICA_ROWS, KVHEADS, HEAD_DIM)
    score_scale = 1.0 / HEAD_DIM ** 0.5
    cache_score = jnp.einsum('rkgd,tkd->kgrt', local_q, cache_keys) * score_scale
    window_score = jnp.einsum('rkgd,skd->kgrs', local_q, window_keys) * score_scale
    positions = jnp.arange(CACHE, dtype=jnp.int32)
    cache_mask = (positions < length)[None, None, None, :]
    row_ids = jnp.arange(REPLICA_ROWS, dtype=jnp.int32)
    same_gram = row_ids[:, None] // NGRAM == row_ids[None, :] // NGRAM
    window_mask = (same_gram & (row_ids[None, :] <= row_ids[:, None]))[None, None]
    cache_score = jnp.where(cache_mask, cache_score, -1e+30)
    window_score = jnp.where(window_mask, window_score, -1e+30)
    row_max = jnp.maximum(lax.optimization_barrier(jnp.max(cache_score, axis=-1)), lax.optimization_barrier(jnp.max(window_score, axis=-1)))[..., None]
    cache_exp = jnp.where(cache_mask, jnp.exp(cache_score - row_max), 0.0)
    window_exp = jnp.where(window_mask, jnp.exp(window_score - row_max), 0.0)
    denom = (lax.optimization_barrier(jnp.sum(cache_exp, axis=-1)) + lax.optimization_barrier(jnp.sum(window_exp, axis=-1)))[..., None]
    cache_prob = (cache_exp / denom).astype(jnp.bfloat16).astype(jnp.float32)
    window_prob = (window_exp / denom).astype(jnp.bfloat16).astype(jnp.float32)
    combined = jnp.einsum('kgrt,tkd->rkgd', cache_prob, cache_vals) + jnp.einsum('kgrs,skd->rkgd', window_prob, window_vals)
    return combined.reshape(REPLICA_ROWS, D).astype(jnp.bfloat16)

def reference(queries, new_kv, cache_kv, cache_len, residual, out_weight, norm_gain, expert_ids, gate_raw, expert_in, expert_out):
    kv_width = KVHEADS * HEAD_DIM
    per_replica = (queries.reshape(N_POOL, REPLICA_ROWS, D), cache_kv[0].reshape(N_POOL, CACHE, kv_width), cache_kv[1].reshape(N_POOL, CACHE, kv_width), new_kv[0].reshape(N_POOL, REPLICA_ROWS, kv_width), new_kv[1].reshape(N_POOL, REPLICA_ROWS, kv_width), cache_len)
    attended = lax.map(lambda items: attend(*items), per_replica).reshape(ROWS_ALL, D)
    projected = jnp.dot(attended, out_weight, preferred_element_type=jnp.float32)
    stream = residual.astype(jnp.float32) + projected
    centre = stream - lax.optimization_barrier(jnp.mean(stream, axis=-1, keepdims=True))
    spread = lax.optimization_barrier(jnp.mean(centre * centre, axis=-1, keepdims=True))
    normed = (centre * lax.rsqrt(spread + 1e-05) * norm_gain).astype(jnp.bfloat16)
    gate_fraction = gate_raw / lax.optimization_barrier(jnp.sum(gate_raw, axis=-1, keepdims=True))
    selected_experts = (expert_ids[:, :, None] == jnp.arange(EXPERTS, dtype=jnp.int32)).astype(jnp.float32)
    member = lax.optimization_barrier(jnp.sum(selected_experts, axis=1))
    weighting = lax.optimization_barrier(jnp.sum(gate_fraction[:, :, None] * selected_experts, axis=1))
    inner_weights = expert_in.reshape(EXPERTS, SLICES, D, FW // SLICES).transpose(0, 2, 1, 3).reshape(EXPERTS, D, FW)
    outer_weights = expert_out.reshape(EXPERTS, FW, D)
    most_rows = N_POOL * N_HEADS * CAP
    row_ids = jnp.arange(ROWS_ALL, dtype=jnp.int32)

    def one_expert(carry, items):
        inner, outer, column = items
        member_col = lax.dynamic_index_in_dim(member, column, axis=1, keepdims=False)
        weight_col = lax.dynamic_index_in_dim(weighting, column, axis=1, keepdims=False)
        sort_keys = jnp.where(member_col > 0, row_ids, row_ids + ROWS_ALL)
        picked = jnp.argsort(sort_keys, stable=True)[:most_rows].astype(jnp.int32)
        taken = normed[picked].astype(jnp.float32).reshape(most_rows, N_HEADS, D // N_HEADS)
        blocks = jnp.einsum('rhf,hfn->rhn', taken, inner.astype(jnp.float32).reshape(N_HEADS, D // N_HEADS, FW))
        blocks = lax.optimization_barrier(blocks.astype(jnp.bfloat16)).astype(jnp.float32)
        pre = lax.optimization_barrier(jnp.sum(blocks, axis=1))
        hidden = jax.nn.silu(pre).astype(jnp.bfloat16)
        result = jnp.dot(hidden, outer, preferred_element_type=jnp.float32)
        scaled = weight_col[picked][:, None] * result
        return (carry.at[picked].add(scaled), None)
    summed, unused = lax.scan(one_expert, jnp.zeros((ROWS_ALL, D), jnp.float32), (inner_weights, outer_weights, jnp.arange(EXPERTS, dtype=jnp.int32)))
    return (stream + summed).astype(jnp.bfloat16)
```

```python
import functools

import jax
import jax.numpy as jnp
import numpy as np
from jax import lax
from jax.experimental import pallas as pl
from jax.experimental.pallas import tpu as pltpu
from jax.sharding import PartitionSpec as P

QHEADS = 48
KVHEADS = 8
HEAD_DIM = 128
EXPERTS = 8
NGRAM = 4
CAP = 3


def row_ids_lower(count):
    row_ids = jnp.arange(count, dtype=jnp.int32)
    return row_ids[:, None] > row_ids[None, :]


def on_device(
    queries,
    new_kv,
    cache_kv,
    cache_len,
    residual,
    out_weight,
    norm_gain,
    expert_ids,
    gate_raw,
    expert_in,
    expert_out,
):
    pool_size = lax.axis_size("pool")
    heads_count = lax.axis_size("heads")
    window_rows = queries.shape[0]
    kv_local = cache_kv.shape[2] // HEAD_DIM
    group = QHEADS // KVHEADS
    width = residual.shape[1]
    local_q = queries.reshape(window_rows, kv_local, group, HEAD_DIM)
    cache_keys = cache_kv[0].reshape(-1, kv_local, HEAD_DIM)
    cache_vals = cache_kv[1].reshape(-1, kv_local, HEAD_DIM)
    window_keys = new_kv[0].reshape(window_rows, kv_local, HEAD_DIM)
    window_vals = new_kv[1].reshape(window_rows, kv_local, HEAD_DIM)
    score_scale = 1.0 / HEAD_DIM**0.5
    cache_score = (
        jnp.einsum("rkgd,tkd->kgrt", local_q, cache_keys, preferred_element_type=jnp.float32)
        * score_scale
    )
    window_score = (
        jnp.einsum("rkgd,skd->kgrs", local_q, window_keys, preferred_element_type=jnp.float32)
        * score_scale
    )
    positions = jnp.arange(cache_keys.shape[0], dtype=jnp.int32)
    cache_mask = (positions < cache_len[0])[None, None, None, :]
    row_ids = jnp.arange(window_rows, dtype=jnp.int32)
    same_gram = row_ids[:, None] // NGRAM == row_ids[None, :] // NGRAM
    window_mask = (same_gram & (row_ids[None, :] <= row_ids[:, None]))[None, None]
    cache_score = jnp.where(cache_mask, cache_score, -1e30)
    window_score = jnp.where(window_mask, window_score, -1e30)
    row_max = jnp.maximum(jnp.max(cache_score, axis=-1), jnp.max(window_score, axis=-1))[..., None]
    cache_exp = jnp.where(cache_mask, jnp.exp(cache_score - row_max), 0.0)
    window_exp = jnp.where(window_mask, jnp.exp(window_score - row_max), 0.0)
    denom = (jnp.sum(cache_exp, axis=-1) + jnp.sum(window_exp, axis=-1))[..., None]
    cache_prob = (cache_exp / denom).astype(jnp.bfloat16)
    window_prob = (window_exp / denom).astype(jnp.bfloat16)
    combined = jnp.einsum(
        "kgrt,tkd->rkgd", cache_prob, cache_vals, preferred_element_type=jnp.float32
    )
    combined = combined + jnp.einsum(
        "kgrs,skd->rkgd", window_prob, window_vals, preferred_element_type=jnp.float32
    )
    attended = combined.reshape(window_rows, -1).astype(jnp.bfloat16)
    partial_value = jnp.dot(
        lax.all_gather(attended, "pool", axis=0, tiled=True),
        out_weight,
        preferred_element_type=jnp.float32,
    )
    partial_value = partial_value.reshape(pool_size, window_rows, -1)
    summed = lax.psum_scatter(
        partial_value.astype(jnp.bfloat16), "heads", scatter_dimension=1, tiled=True
    ).astype(jnp.float32)
    projected = lax.all_to_all(
        summed.astype(jnp.bfloat16), "pool", split_axis=0, concat_axis=2, tiled=True
    ).astype(summed.dtype)[0]
    stream = residual.astype(jnp.float32) + projected
    centre = stream - jnp.mean(stream, axis=-1, keepdims=True)
    spread = jnp.mean(centre * centre, axis=-1, keepdims=True)
    normed = (centre * lax.rsqrt(spread + 1e-05) * norm_gain).astype(jnp.bfloat16)
    resident_rows = normed.shape[0]
    slices = max(pool_size // EXPERTS, 1)
    local_count = expert_in.shape[0]
    slot_count = CAP
    owner_index = np.arange(local_count * pool_size)
    owner_expert = (owner_index % pool_size * local_count + owner_index // pool_size) // slices
    expert_owner_lookup = jnp.asarray(
        (owner_expert[:, None] == np.arange(EXPERTS)[None, :]).astype(np.float32)
    )
    selected_experts = (expert_ids[:, :, None] == jnp.arange(EXPERTS, dtype=jnp.int32)).astype(
        jnp.float32
    )
    member = jnp.sum(selected_experts, axis=1)
    before = row_ids_lower(resident_rows).astype(jnp.float32)
    rank_rows = jnp.dot(
        before, member, precision=lax.Precision.HIGHEST, preferred_element_type=jnp.float32
    )
    slot_index = jnp.sum(selected_experts * rank_rows[:, None, :], axis=2)
    slot_onehot_mask = (slot_index[:, :, None] == jnp.arange(slot_count, dtype=jnp.float32)).astype(
        jnp.float32
    )
    expert_location = jnp.einsum("vyu,vyt->vut", selected_experts, slot_onehot_mask)
    dispatch_table = jnp.einsum("ydr,ad->ary", expert_location, expert_owner_lookup).astype(
        jnp.bfloat16
    )
    sending = jnp.einsum(
        "jci,id->jcd", dispatch_table, normed, preferred_element_type=jnp.float32
    ).astype(jnp.bfloat16)
    outgoing = sending.reshape(
        local_count, pool_size, slot_count, heads_count, width // heads_count
    )
    received = lax.all_to_all(
        lax.all_to_all(outgoing, "pool", split_axis=1, concat_axis=1, tiled=True),
        "heads",
        split_axis=3,
        concat_axis=3,
        tiled=True,
    )
    routed_rows = pool_size * slot_count * heads_count
    rows_in = received.reshape(local_count, routed_rows, width // heads_count)
    pre_part = jnp.einsum("lmf,lfn->lmn", rows_in, expert_in, preferred_element_type=jnp.float32)
    hidden_total = lax.psum(pre_part.astype(jnp.bfloat16), "heads").astype(jnp.float32)
    hidden = jax.nn.silu(hidden_total).astype(jnp.bfloat16)
    result = jnp.einsum("lmn,lnd->lmd", hidden, expert_out, preferred_element_type=jnp.float32)
    result = result.reshape(local_count, pool_size, slot_count, heads_count, -1)
    gate_fraction = gate_raw / jnp.sum(gate_raw, axis=-1, keepdims=True)
    gate_scaled_output = jnp.einsum(
        "qv,qvg,qvr->qgr", gate_fraction, selected_experts, slot_onehot_mask
    )
    returned = lax.all_to_all(
        lax.all_to_all(
            result.astype(jnp.bfloat16), "pool", split_axis=1, concat_axis=1, tiled=True
        ),
        "heads",
        split_axis=3,
        concat_axis=3,
        tiled=True,
    ).astype(result.dtype)
    returned_flat = returned.reshape(local_count * pool_size * slot_count, width)
    merge_weight_table = jnp.einsum("gbu,db->gdu", gate_scaled_output, expert_owner_lookup).reshape(
        resident_rows, -1
    )
    expert_sum = jnp.dot(
        merge_weight_table,
        returned_flat,
        precision=lax.Precision.HIGHEST,
        preferred_element_type=jnp.float32,
    )
    return (stream + expert_sum).astype(jnp.bfloat16)


MESH = pl.DeviceIdType.MESH
VMEM_LIMIT = 62 * 2**20
CHUNKS = 6
OUT_SLOTS = 3


def dot(lhs, rhs):
    return jnp.dot(lhs, rhs, preferred_element_type=jnp.float32)


def fused_kernel(
    sizes,
    q_ref,
    nkv_ref,
    cache_ref,
    len_ref,
    res_ref,
    ow_ref,
    gain_ref,
    ids_ref,
    raw_ref,
    ein_ref,
    eout_ref,
    out_ref,
    cache_v,
    ow_v,
    ein_v,
    eout_v,
    gate_tile,
    gate_land,
    gate_rows,
    att,
    big,
    packed,
    msg_a,
    land_a,
    stream,
    gain_s,
    msg_b,
    land_b,
    rows_bf,
    own,
    a_send,
    a_land,
    b_send,
    b_land,
    hid,
    acc,
    msg_c,
    land_c,
    flat,
    s_cache,
    s_ow,
    s_ein,
    s_eout,
    g_s,
    g_r,
    t_s,
    t_r,
    a_s,
    a_r,
    b_s,
    b_r,
    c_s,
    c_r,
    ha_s,
    ha_r,
    hb_s,
    hb_r,
    hc_s,
    hc_r,
):
    pools, heads, owned, chunks, width = sizes
    devices = pools * heads
    window = q_ref.shape[0]
    all_rows = devices * owned
    parts = window // owned
    block = ow_ref.shape[1]
    piece = block // parts
    p = lax.axis_index("pool")
    h = lax.axis_index("heads")
    me = p * heads + h
    core = h % 2
    sibling = (h // 2) * 2 + (1 - core)
    across = (h + 2) % heads

    def dev(flat_id):
        return {"pool": flat_id // heads, "heads": flat_id % heads}

    cache_copy = pltpu.make_async_copy(cache_ref, cache_v, s_cache)
    cache_copy.start()
    ow_copy = pltpu.make_async_copy(ow_ref, ow_v, s_ow)
    ow_copy.start()

    def ein_copy(k):
        at = pl.ds(pl.multiple_of(k * width, width), width)
        return pltpu.make_async_copy(ein_ref.at[:, :, at], ein_v.at[k], s_ein.at[k])

    def eout_copy(k):
        at = pl.ds(pl.multiple_of(k * width, width), width)
        return pltpu.make_async_copy(
            eout_ref.at[:, at, :], eout_v.at[k % OUT_SLOTS], s_eout.at[k]
        )

    for k in range(chunks):
        ein_copy(k).start()
    for k in range(OUT_SLOTS):
        eout_copy(k).start()

    barrier = pltpu.get_barrier_semaphore()

    @pl.loop(1, devices)
    def _(d):
        pl.semaphore_signal(
            barrier, inc=1, device_id=dev((me + d) % devices), device_id_type=MESH
        )

    pl.semaphore_wait(barrier, devices - 1)

    def exchange(source, land, send, recv, start):
        @pl.loop(1, devices)
        def _(d):
            to = (me + d) % devices
            copy = pltpu.make_async_remote_copy(
                src_ref=source(to),
                dst_ref=land.at[me],
                send_sem=send.at[d],
                recv_sem=recv.at[d],
                device_id=dev(to),
                device_id_type=MESH,
            )
            if start == 0:
                copy.start()
            elif start == 1:
                copy.wait_recv()
            else:
                copy.wait_send()

    ids = ids_ref[...]
    raw = raw_ref[...]
    share = raw / jnp.sum(raw, axis=-1, keepdims=True)
    lane = lax.broadcasted_iota(jnp.int32, (owned, 128), 1)
    table = jnp.zeros((owned, 128), jnp.float32)
    for v in range(ids_ref.shape[1]):
        table = table + jnp.where(lane == ids[:, v : v + 1], share[:, v : v + 1], 0.0)
    gate_tile[...] = jnp.zeros_like(gate_tile)
    gate_tile[0:owned, :] = table

    def gate_src(to):
        return gate_tile

    exchange(gate_src, gate_land, g_s, g_r, 0)
    gate_land[me] = gate_tile[...]

    residual = res_ref[...].astype(jnp.float32)
    for b in range(pools):
        for j in range(parts):
            at = (b * parts + j) * piece
            rows = slice(j * owned, (j + 1) * owned)
            stream[b, rows, :] = residual[:, at : at + piece]
            gain_s[b, rows, :] = jnp.broadcast_to(gain_ref[:, at : at + piece], (owned, piece))

    cache_copy.wait()
    kv_local = cache_ref.shape[2] // HEAD_DIM
    group = q_ref.shape[1] // HEAD_DIM // kv_local
    cached = cache_ref.shape[1]
    scale = 1.0 / HEAD_DIM**0.5
    length = len_ref[0]
    stacked = group * window
    cache_mask = lax.broadcasted_iota(jnp.int32, (stacked, cached), 1) < length
    row = lax.broadcasted_iota(jnp.int32, (stacked, window), 0) % window
    col = lax.broadcasted_iota(jnp.int32, (stacked, window), 1)
    window_mask = (row // NGRAM == col // NGRAM) & (col <= row)
    contract = (((1,), (1,)), ((), ()))
    for k in range(kv_local):
        at = slice(k * HEAD_DIM, (k + 1) * HEAD_DIM)
        q = jnp.concatenate(
            [
                q_ref[:, (k * group + g) * HEAD_DIM : (k * group + g + 1) * HEAD_DIM]
                for g in range(group)
            ],
            axis=0,
        )
        s_c = lax.dot_general(q, cache_v[0, :, at], contract, preferred_element_type=jnp.float32)
        s_w = lax.dot_general(q, nkv_ref[0, :, at], contract, preferred_element_type=jnp.float32)
        s_c = jnp.where(cache_mask, s_c * scale, -1e30)
        s_w = jnp.where(window_mask, s_w * scale, -1e30)
        top = jnp.maximum(
            jnp.max(s_c, axis=-1, keepdims=True), jnp.max(s_w, axis=-1, keepdims=True)
        )
        e_c = jnp.where(cache_mask, jnp.exp(s_c - top), 0.0)
        e_w = jnp.where(window_mask, jnp.exp(s_w - top), 0.0)
        inv = 1.0 / (
            jnp.sum(e_c, axis=-1, keepdims=True) + jnp.sum(e_w, axis=-1, keepdims=True)
        )
        o = dot((e_c * inv).astype(jnp.bfloat16), cache_v[1, :, at])
        o = o + dot((e_w * inv).astype(jnp.bfloat16), nkv_ref[1, :, at])
        o = o.astype(jnp.bfloat16)
        for g in range(group):
            att[p, :, (k * group + g) * HEAD_DIM : (k * group + g + 1) * HEAD_DIM] = o[
                g * window : (g + 1) * window
            ]

    def att_copy(d):
        return pltpu.make_async_remote_copy(
            src_ref=att.at[p],
            dst_ref=att.at[p],
            send_sem=t_s.at[d],
            recv_sem=t_r.at[d],
            device_id={"pool": (p + d) % pools, "heads": h},
            device_id_type=MESH,
        )

    for d in range(1, pools):
        att_copy(d).start()
    for d in range(1, pools):
        att_copy(d).wait_recv()
    ow_copy.wait()
    gathered = jnp.concatenate([att[b] for b in range(pools)], axis=0)
    big[...] = dot(gathered, ow_v[...])

    def pack_into(msg):
        for t in range(devices):
            for j in range(parts):
                packed[t, j * owned : (j + 1) * owned, :] = big[
                    t * owned : (t + 1) * owned, j * piece : (j + 1) * piece
                ]
        msg[...] = packed[...].astype(jnp.bfloat16)

    pack_into(msg_a)
    exchange(lambda to: msg_a.at[to], land_a, a_s, a_r, 0)
    land_a[me] = msg_a[me]
    exchange(lambda to: msg_a.at[to], land_a, a_s, a_r, 1)

    total = jnp.zeros((window, 1), jnp.float32)
    for b in range(pools):
        x = stream[b]
        for i in range(heads):
            x = x + land_a[b * heads + i].astype(jnp.float32)
        stream[b] = x
        total = total + jnp.sum(x, axis=-1, keepdims=True)

    def over_parts(column):
        wide = jnp.broadcast_to(column, (window, 128))
        out = wide
        for j in range(1, parts):
            out = out + pltpu.roll(wide, j * owned, 0)
        return out[:, 0:1]

    full = pools * block
    mean = over_parts(total) * (1.0 / full)
    square = jnp.zeros((window, 1), jnp.float32)
    for b in range(pools):
        centre = stream[b] - mean
        square = square + jnp.sum(centre * centre, axis=-1, keepdims=True)
    inv_std = lax.rsqrt(over_parts(square) * (1.0 / full) + 1e-05)
    for b in range(pools):
        msg_b[b] = ((stream[b] - mean) * inv_std * gain_s[b]).astype(jnp.bfloat16)

    exchange(lambda to: msg_b.at[to % heads], land_b, b_s, b_r, 0)
    land_b[me] = msg_b[h]
    exchange(gate_src, gate_land, g_s, g_r, 1)
    for t in range(devices):
        gate_rows[t * owned : (t + 1) * owned, :] = gate_land[t, 0:owned, :]
    exchange(lambda to: msg_b.at[to % heads], land_b, b_s, b_r, 1)
    for t in range(devices):
        x = land_b[t].astype(jnp.float32)
        for j in range(parts):
            big[t * owned : (t + 1) * owned, j * piece : (j + 1) * piece] = x[
                j * owned : (j + 1) * owned
            ]
    rows_bf[...] = big[...].astype(jnp.bfloat16)

    def hop(source, land, send, recv, k, to):
        return pltpu.make_async_remote_copy(
            src_ref=source,
            dst_ref=land,
            send_sem=send.at[k],
            recv_sem=recv.at[k],
            device_id={"pool": p, "heads": to},
            device_id_type=MESH,
        )

    def hop_a(k):
        return hop(a_send.at[k], a_land.at[k], ha_s, ha_r, k, sibling)

    def hop_b(k):
        return hop(b_send.at[k], b_land.at[k], hb_s, hb_r, k, across)

    def hop_c(k):
        return hop(hid.at[k, core], hid.at[k, core], hc_s, hc_r, k, sibling)

    acc[...] = jnp.zeros_like(acc)

    @pl.loop(0, chunks + 3)
    def _(i):
        @pl.when((i >= 1) & (i < chunks + 1))
        def _():
            k = i - 1
            hop_a(k).wait_recv()
            b_send[k] = (own[k % 2] + a_land[k].astype(jnp.float32)).astype(jnp.bfloat16)
            hop_b(k).start()

        @pl.when(i < chunks)
        def _():
            ein_copy(i).wait()
            a_send[i] = dot(rows_bf[...], ein_v[i, 1 - core]).astype(jnp.bfloat16)
            hop_a(i).start()
            own[i % 2] = dot(rows_bf[...], ein_v[i, core])

        @pl.when((i >= 2) & (i < chunks + 2))
        def _():
            k = i - 2
            hop_b(k).wait_recv()
            pre = b_send[k].astype(jnp.float32) + b_land[k].astype(jnp.float32)
            hid[k, core] = (pre / (1.0 + jnp.exp(-pre))).astype(jnp.bfloat16)
            hop_c(k).start()

        @pl.when(i >= 3)
        def _():
            k = i - 3
            eout_copy(k).wait()
            slot = k % OUT_SLOTS
            acc[core] += dot(hid[k, core], eout_v[slot, core])
            hop_c(k).wait_recv()
            acc[1 - core] += dot(hid[k, 1 - core], eout_v[slot, 1 - core])

            @pl.when(k + OUT_SLOTS < chunks)
            def _():
                eout_copy(k + OUT_SLOTS).start()

    lanes = lax.broadcasted_iota(jnp.int32, (all_rows, 128), 1)
    result = jnp.zeros((all_rows, block), jnp.float32)
    for l in range(2):
        weight = jnp.sum(
            jnp.where(lanes == p * 2 + l, gate_rows[...], 0.0), axis=-1, keepdims=True
        )
        result = result + weight * acc[l]
    big[...] = result
    pack_into(msg_c)
    exchange(lambda to: msg_c.at[to], land_c, c_s, c_r, 0)
    land_c[me] = msg_c[me]
    exchange(lambda to: msg_c.at[to], land_c, c_s, c_r, 1)
    for i in range(heads):
        x = stream[i]
        for b in range(pools):
            x = x + land_c[b * heads + i].astype(jnp.float32)
        for j in range(parts):
            at = (i * parts + j) * piece
            flat[:, at : at + piece] = x[j * owned : (j + 1) * owned]
    out_ref[...] = flat[...].astype(out_ref.dtype)

    exchange(gate_src, gate_land, g_s, g_r, 2)
    for d in range(1, pools):
        att_copy(d).wait_send()
    exchange(lambda to: msg_a.at[to], land_a, a_s, a_r, 2)
    exchange(lambda to: msg_b.at[to % heads], land_b, b_s, b_r, 2)
    exchange(lambda to: msg_c.at[to], land_c, c_s, c_r, 2)

    @pl.loop(0, chunks)
    def _(k):
        hop_a(k).wait_send()
        hop_b(k).wait_send()
        hop_c(k).wait_send()


def fused(queries, new_kv, cache_kv, cache_len, residual, out_weight, norm_gain, expert_ids, gate_raw, expert_in, expert_out):
    pools, heads = lax.axis_size("pool"), lax.axis_size("heads")
    owned, features = residual.shape
    local, depth, hidden = expert_in.shape
    devices = pools * heads
    chunks = CHUNKS
    width = hidden // chunks
    window = queries.shape[0]
    all_rows = devices * owned
    block = out_weight.shape[1]
    piece = block * owned // window
    bf, f32 = jnp.bfloat16, jnp.float32
    vmem = pl.BlockSpec(memory_space=pltpu.VMEM)
    hbm = pl.BlockSpec(memory_space=pl.ANY)
    smem = pl.BlockSpec(memory_space=pltpu.SMEM)
    dma = pltpu.SemaphoreType.DMA
    msgs = (devices, window, piece)
    return pl.pallas_call(
        functools.partial(fused_kernel, (pools, heads, owned, chunks, width)),
        out_shape=jax.ShapeDtypeStruct((owned, features), bf),
        in_specs=[vmem, vmem, hbm, smem, vmem, hbm, vmem, vmem, vmem, hbm, hbm],
        out_specs=vmem,
        scratch_shapes=[
            pltpu.VMEM(cache_kv.shape, bf),
            pltpu.VMEM(out_weight.shape, bf),
            pltpu.VMEM((chunks, local, depth, width), bf),
            pltpu.VMEM((OUT_SLOTS, local, width, block), bf),
            pltpu.VMEM((8, 128), f32),
            pltpu.VMEM((devices, 8, 128), f32),
            pltpu.VMEM((all_rows, 128), f32),
            pltpu.VMEM((pools, window, queries.shape[1]), bf),
            pltpu.VMEM((all_rows, block), f32),
            pltpu.VMEM(msgs, f32),
            pltpu.VMEM(msgs, bf),
            pltpu.VMEM(msgs, bf),
            pltpu.VMEM((pools, window, piece), f32),
            pltpu.VMEM((pools, window, piece), f32),
            pltpu.VMEM((heads, window, piece), bf),
            pltpu.VMEM(msgs, bf),
            pltpu.VMEM((all_rows, block), bf),
            pltpu.VMEM((2, all_rows, width), f32),
            pltpu.VMEM((chunks, all_rows, width), bf),
            pltpu.VMEM((chunks, all_rows, width), bf),
            pltpu.VMEM((chunks, all_rows, width), bf),
            pltpu.VMEM((chunks, all_rows, width), bf),
            pltpu.VMEM((chunks, local, all_rows, width), bf),
            pltpu.VMEM((local, all_rows, block), f32),
            pltpu.VMEM(msgs, bf),
            pltpu.VMEM(msgs, bf),
            pltpu.VMEM((owned, features), f32),
            dma,
            dma,
            dma((chunks,)),
            dma((chunks,)),
            dma((devices,)),
            dma((devices,)),
            dma((pools,)),
            dma((pools,)),
            dma((devices,)),
            dma((devices,)),
            dma((devices,)),
            dma((devices,)),
            dma((devices,)),
            dma((devices,)),
            dma((chunks,)),
            dma((chunks,)),
            dma((chunks,)),
            dma((chunks,)),
            dma((chunks,)),
            dma((chunks,)),
        ],
        compiler_params=pltpu.CompilerParams(
            collective_id=0, has_side_effects=True, vmem_limit_bytes=VMEM_LIMIT
        ),
    )(queries, new_kv, cache_kv, cache_len, residual, out_weight, norm_gain.reshape(1, -1), expert_ids, gate_raw, expert_in, expert_out)


def one_kernel(mesh, *args):
    queries, residual, out_weight, expert_in = args[0], args[4], args[5], args[9]
    pools, heads = mesh.shape["pool"], mesh.shape["heads"]
    window, owned, block = queries.shape[0], residual.shape[0], out_weight.shape[1]
    local, depth, hidden = expert_in.shape
    return (
        pools == heads
        and heads == 4
        and local == 2
        and pools * local == EXPERTS
        and window == heads * owned
        and window % 16 == 0
        and depth == block
        and block % (heads * 128) == 0
        and hidden % (CHUNKS * 128) == 0
    )


def solution(mesh):
    placed = (
        P(("groups", "pool"), "heads"),
        P(None, ("groups", "pool"), "heads"),
        P(None, ("groups", "pool"), "heads"),
        P(("groups", "pool")),
        P(("groups", "pool", "heads"), None),
        P("heads", "pool"),
        P(),
        P(("groups", "pool", "heads"), None),
        P(("groups", "pool", "heads"), None),
        P("pool", "heads", None),
        P("pool", None, "heads"),
    )
    def on_blocks(*args):
        if one_kernel(mesh, *args):
            return fused(*args)
        return on_device(*args)

    return jax.shard_map(
        on_blocks,
        mesh=mesh,
        in_specs=placed,
        out_specs=P(("groups", "pool", "heads"), None),
        check_vma=False,
    )
```

```python
import functools

import jax
import jax.numpy as jnp
import numpy as np
from jax import lax
from jax.experimental import pallas as pl
from jax.experimental.pallas import tpu as pltpu
from jax.sharding import PartitionSpec as P

QHEADS = 48
KVHEADS = 8
HEAD_DIM = 128
EXPERTS = 8
NGRAM = 4
CAP = 3


def row_ids_lower(count):
    row_ids = jnp.arange(count, dtype=jnp.int32)
    return row_ids[:, None] > row_ids[None, :]


def on_device(
    queries,
    new_kv,
    cache_kv,
    cache_len,
    residual,
    out_weight,
    norm_gain,
    expert_ids,
    gate_raw,
    expert_in,
    expert_out,
):
    pool_size = lax.axis_size("pool")
    heads_count = lax.axis_size("heads")
    window_rows = queries.shape[0]
    kv_local = cache_kv.shape[2] // HEAD_DIM
    group = QHEADS // KVHEADS
    width = residual.shape[1]
    local_q = queries.reshape(window_rows, kv_local, group, HEAD_DIM)
    cache_keys = cache_kv[0].reshape(-1, kv_local, HEAD_DIM)
    cache_vals = cache_kv[1].reshape(-1, kv_local, HEAD_DIM)
    window_keys = new_kv[0].reshape(window_rows, kv_local, HEAD_DIM)
    window_vals = new_kv[1].reshape(window_rows, kv_local, HEAD_DIM)
    score_scale = 1.0 / HEAD_DIM**0.5
    cache_score = (
        jnp.einsum("rkgd,tkd->kgrt", local_q, cache_keys, preferred_element_type=jnp.float32)
        * score_scale
    )
    window_score = (
        jnp.einsum("rkgd,skd->kgrs", local_q, window_keys, preferred_element_type=jnp.float32)
        * score_scale
    )
    positions = jnp.arange(cache_keys.shape[0], dtype=jnp.int32)
    cache_mask = (positions < cache_len[0])[None, None, None, :]
    row_ids = jnp.arange(window_rows, dtype=jnp.int32)
    same_gram = row_ids[:, None] // NGRAM == row_ids[None, :] // NGRAM
    window_mask = (same_gram & (row_ids[None, :] <= row_ids[:, None]))[None, None]
    cache_score = jnp.where(cache_mask, cache_score, -1e30)
    window_score = jnp.where(window_mask, window_score, -1e30)
    row_max = jnp.maximum(jnp.max(cache_score, axis=-1), jnp.max(window_score, axis=-1))[..., None]
    cache_exp = jnp.where(cache_mask, jnp.exp(cache_score - row_max), 0.0)
    window_exp = jnp.where(window_mask, jnp.exp(window_score - row_max), 0.0)
    denom = (jnp.sum(cache_exp, axis=-1) + jnp.sum(window_exp, axis=-1))[..., None]
    cache_prob = (cache_exp / denom).astype(jnp.bfloat16)
    window_prob = (window_exp / denom).astype(jnp.bfloat16)
    combined = jnp.einsum(
        "kgrt,tkd->rkgd", cache_prob, cache_vals, preferred_element_type=jnp.float32
    )
    combined = combined + jnp.einsum(
        "kgrs,skd->rkgd", window_prob, window_vals, preferred_element_type=jnp.float32
    )
    attended = combined.reshape(window_rows, -1).astype(jnp.bfloat16)
    partial_value = jnp.dot(
        lax.all_gather(attended, "pool", axis=0, tiled=True),
        out_weight,
        preferred_element_type=jnp.float32,
    )
    partial_value = partial_value.reshape(pool_size, window_rows, -1)
    summed = lax.psum_scatter(
        partial_value.astype(jnp.bfloat16), "heads", scatter_dimension=1, tiled=True
    ).astype(jnp.float32)
    projected = lax.all_to_all(
        summed.astype(jnp.bfloat16), "pool", split_axis=0, concat_axis=2, tiled=True
    ).astype(summed.dtype)[0]
    stream = residual.astype(jnp.float32) + projected
    centre = stream - jnp.mean(stream, axis=-1, keepdims=True)
    spread = jnp.mean(centre * centre, axis=-1, keepdims=True)
    normed = (centre * lax.rsqrt(spread + 1e-05) * norm_gain).astype(jnp.bfloat16)
    resident_rows = normed.shape[0]
    slices = max(pool_size // EXPERTS, 1)
    local_count = expert_in.shape[0]
    slot_count = CAP
    owner_index = np.arange(local_count * pool_size)
    owner_expert = (owner_index % pool_size * local_count + owner_index // pool_size) // slices
    expert_owner_lookup = jnp.asarray(
        (owner_expert[:, None] == np.arange(EXPERTS)[None, :]).astype(np.float32)
    )
    selected_experts = (expert_ids[:, :, None] == jnp.arange(EXPERTS, dtype=jnp.int32)).astype(
        jnp.float32
    )
    member = jnp.sum(selected_experts, axis=1)
    before = row_ids_lower(resident_rows).astype(jnp.float32)
    rank_rows = jnp.dot(
        before, member, precision=lax.Precision.HIGHEST, preferred_element_type=jnp.float32
    )
    slot_index = jnp.sum(selected_experts * rank_rows[:, None, :], axis=2)
    slot_onehot_mask = (slot_index[:, :, None] == jnp.arange(slot_count, dtype=jnp.float32)).astype(
        jnp.float32
    )
    expert_location = jnp.einsum("vyu,vyt->vut", selected_experts, slot_onehot_mask)
    dispatch_table = jnp.einsum("ydr,ad->ary", expert_location, expert_owner_lookup).astype(
        jnp.bfloat16
    )
    sending = jnp.einsum(
        "jci,id->jcd", dispatch_table, normed, preferred_element_type=jnp.float32
    ).astype(jnp.bfloat16)
    outgoing = sending.reshape(
        local_count, pool_size, slot_count, heads_count, width // heads_count
    )
    received = lax.all_to_all(
        lax.all_to_all(outgoing, "pool", split_axis=1, concat_axis=1, tiled=True),
        "heads",
        split_axis=3,
        concat_axis=3,
        tiled=True,
    )
    routed_rows = pool_size * slot_count * heads_count
    rows_in = received.reshape(local_count, routed_rows, width // heads_count)
    pre_part = jnp.einsum("lmf,lfn->lmn", rows_in, expert_in, preferred_element_type=jnp.float32)
    hidden_total = lax.psum(pre_part.astype(jnp.bfloat16), "heads").astype(jnp.float32)
    hidden = jax.nn.silu(hidden_total).astype(jnp.bfloat16)
    result = jnp.einsum("lmn,lnd->lmd", hidden, expert_out, preferred_element_type=jnp.float32)
    result = result.reshape(local_count, pool_size, slot_count, heads_count, -1)
    gate_fraction = gate_raw / jnp.sum(gate_raw, axis=-1, keepdims=True)
    gate_scaled_output = jnp.einsum(
        "qv,qvg,qvr->qgr", gate_fraction, selected_experts, slot_onehot_mask
    )
    returned = lax.all_to_all(
        lax.all_to_all(
            result.astype(jnp.bfloat16), "pool", split_axis=1, concat_axis=1, tiled=True
        ),
        "heads",
        split_axis=3,
        concat_axis=3,
        tiled=True,
    ).astype(result.dtype)
    returned_flat = returned.reshape(local_count * pool_size * slot_count, width)
    merge_weight_table = jnp.einsum("gbu,db->gdu", gate_scaled_output, expert_owner_lookup).reshape(
        resident_rows, -1
    )
    expert_sum = jnp.dot(
        merge_weight_table,
        returned_flat,
        precision=lax.Precision.HIGHEST,
        preferred_element_type=jnp.float32,
    )
    return (stream + expert_sum).astype(jnp.bfloat16)


MESH = pl.DeviceIdType.MESH
VMEM_LIMIT = 62 * 2**20
SLOTS = 11


def dot(lhs, rhs):
    return jnp.dot(lhs, rhs, preferred_element_type=jnp.float32)


def fused_kernel(
    sizes,
    q_ref,
    nkv_ref,
    cache_ref,
    len_ref,
    res_ref,
    ow_ref,
    gain_ref,
    ids_ref,
    raw_ref,
    ein_ref,
    eout_ref,
    out_ref,
    cache_v,
    wts,
    gate_tile,
    gate_land,
    gate_rows,
    att,
    big,
    packed,
    msg_a,
    land_a,
    stream,
    gain_s,
    msg_b,
    land_b,
    rows_bf,
    merge,
    own,
    a_send,
    a_land,
    b_send,
    b_land,
    hid,
    acc,
    msg_c,
    land_c,
    flat,
    s_cache,
    s_ow,
    s_ein,
    s_eout,
    g_s,
    g_r,
    t_s,
    t_r,
    a_s,
    a_r,
    b_s,
    b_r,
    c_s,
    c_r,
    ha_s,
    ha_r,
    hb_s,
    hb_r,
    hc_s,
    hc_r,
):
    pools, heads, owned, chunks, width, cap = sizes
    devices = pools * heads
    window = q_ref.shape[0]
    all_rows = devices * owned
    parts = window // owned
    block = ow_ref.shape[1]
    piece = block // parts
    p = lax.axis_index("pool")
    h = lax.axis_index("heads")
    me = p * heads + h
    core = h % 2
    sibling = (h // 2) * 2 + (1 - core)
    across = (h + 2) % heads

    def dev(flat_id):
        return {"pool": flat_id // heads, "heads": flat_id % heads}

    cache_copy = pltpu.make_async_copy(cache_ref, cache_v, s_cache)
    cache_copy.start()

    def span(k):
        return pl.ds(pl.multiple_of(k * width, width), width)

    def ow_copies():
        return [
            pltpu.make_async_copy(
                ow_ref.at[span(a), span(b)], wts.at[0, a, b], s_ow.at[a, b]
            )
            for a in range(2)
            for b in range(2)
        ]

    def ein_slot(k):
        return (1 + k) % SLOTS

    def eout_slot(k):
        return (1 + chunks + k) % SLOTS

    def ein_copies(k):
        return [
            pltpu.make_async_copy(
                ein_ref.at[:, span(a), span(k)], wts.at[ein_slot(k), :, a], s_ein.at[k, a]
            )
            for a in range(2)
        ]

    def eout_copies(k):
        return [
            pltpu.make_async_copy(
                eout_ref.at[:, span(k), span(a)], wts.at[eout_slot(k), :, a], s_eout.at[k, a]
            )
            for a in range(2)
        ]

    def start(copies):
        for copy in copies:
            copy.start()

    def wait(copies):
        for copy in copies:
            copy.wait()

    ahead = SLOTS - 1 - chunks
    start(ow_copies())

    barrier = pltpu.get_barrier_semaphore()

    @pl.loop(1, devices)
    def _(d):
        pl.semaphore_signal(
            barrier, inc=1, device_id=dev((me + d) % devices), device_id_type=MESH
        )

    pl.semaphore_wait(barrier, devices - 1)

    def exchange(source, land, send, recv, step):
        @pl.loop(1, devices)
        def _(d):
            to = (me + d) % devices
            copy = pltpu.make_async_remote_copy(
                src_ref=source(to),
                dst_ref=land.at[me],
                send_sem=send.at[d],
                recv_sem=recv.at[d],
                device_id=dev(to),
                device_id_type=MESH,
            )
            if step == 0:
                copy.start()
            elif step == 1:
                copy.wait_recv()
            else:
                copy.wait_send()

    ids = ids_ref[...]
    raw = raw_ref[...]
    share = raw / jnp.sum(raw, axis=-1, keepdims=True)
    lane = lax.broadcasted_iota(jnp.int32, (owned, 128), 1)
    table = jnp.zeros((owned, 128), jnp.float32)
    for v in range(ids_ref.shape[1]):
        table = table + jnp.where(lane == ids[:, v : v + 1], share[:, v : v + 1], 0.0)
    gate_tile[...] = jnp.zeros_like(gate_tile)
    gate_tile[0:owned, :] = table

    def gate_src(to):
        return gate_tile

    exchange(gate_src, gate_land, g_s, g_r, 0)
    gate_land[me] = gate_tile[...]

    residual = res_ref[...].astype(jnp.float32)
    for b in range(pools):
        for j in range(parts):
            at = (b * parts + j) * piece
            rows = slice(j * owned, (j + 1) * owned)
            stream[b, rows, :] = residual[:, at : at + piece]
            gain_s[b, rows, :] = jnp.broadcast_to(gain_ref[:, at : at + piece], (owned, piece))

    cache_copy.wait()
    for k in range(chunks):
        start(ein_copies(k))
    for k in range(ahead):
        start(eout_copies(k))
    kv_local = cache_ref.shape[2] // HEAD_DIM
    group = q_ref.shape[1] // HEAD_DIM // kv_local
    cached = cache_ref.shape[1]
    scale = 1.0 / HEAD_DIM**0.5
    length = len_ref[0]
    stacked = group * window
    cache_mask = lax.broadcasted_iota(jnp.int32, (stacked, cached), 1) < length
    row = lax.broadcasted_iota(jnp.int32, (stacked, window), 0) % window
    col = lax.broadcasted_iota(jnp.int32, (stacked, window), 1)
    window_mask = (row // NGRAM == col // NGRAM) & (col <= row)
    contract = (((1,), (1,)), ((), ()))
    for k in range(kv_local):
        at = slice(k * HEAD_DIM, (k + 1) * HEAD_DIM)
        q = jnp.concatenate(
            [
                q_ref[:, (k * group + g) * HEAD_DIM : (k * group + g + 1) * HEAD_DIM]
                for g in range(group)
            ],
            axis=0,
        )
        s_c = lax.dot_general(q, cache_v[0, :, at], contract, preferred_element_type=jnp.float32)
        s_w = lax.dot_general(q, nkv_ref[0, :, at], contract, preferred_element_type=jnp.float32)
        s_c = jnp.where(cache_mask, s_c * scale, -1e30)
        s_w = jnp.where(window_mask, s_w * scale, -1e30)
        top = jnp.maximum(
            jnp.max(s_c, axis=-1, keepdims=True), jnp.max(s_w, axis=-1, keepdims=True)
        )
        e_c = jnp.where(cache_mask, jnp.exp(s_c - top), 0.0)
        e_w = jnp.where(window_mask, jnp.exp(s_w - top), 0.0)
        inv = 1.0 / (
            jnp.sum(e_c, axis=-1, keepdims=True) + jnp.sum(e_w, axis=-1, keepdims=True)
        )
        o = dot((e_c * inv).astype(jnp.bfloat16), cache_v[1, :, at])
        o = o + dot((e_w * inv).astype(jnp.bfloat16), nkv_ref[1, :, at])
        o = o.astype(jnp.bfloat16)
        for g in range(group):
            att[p, :, (k * group + g) * HEAD_DIM : (k * group + g + 1) * HEAD_DIM] = o[
                g * window : (g + 1) * window
            ]

    def att_copy(d):
        return pltpu.make_async_remote_copy(
            src_ref=att.at[p],
            dst_ref=att.at[p],
            send_sem=t_s.at[d],
            recv_sem=t_r.at[d],
            device_id={"pool": (p + d) % pools, "heads": h},
            device_id_type=MESH,
        )

    for d in range(1, pools):
        att_copy(d).start()
    for d in range(1, pools):
        att_copy(d).wait_recv()
    wait(ow_copies())
    gathered = jnp.concatenate([att[b] for b in range(pools)], axis=0)
    for b in range(2):
        big[:, b * width : (b + 1) * width] = dot(gathered[:, :width], wts[0, 0, b]) + dot(
            gathered[:, width:], wts[0, 1, b]
        )
    start(eout_copies(ahead))

    def pack_into(msg):
        for t in range(devices):
            for j in range(parts):
                packed[t, j * owned : (j + 1) * owned, :] = big[
                    t * owned : (t + 1) * owned, j * piece : (j + 1) * piece
                ]
        msg[...] = packed[...].astype(jnp.bfloat16)

    pack_into(msg_a)
    exchange(lambda to: msg_a.at[to], land_a, a_s, a_r, 0)
    land_a[me] = msg_a[me]
    exchange(lambda to: msg_a.at[to], land_a, a_s, a_r, 1)

    total = jnp.zeros((window, 1), jnp.float32)
    for b in range(pools):
        x = stream[b]
        for i in range(heads):
            x = x + land_a[b * heads + i].astype(jnp.float32)
        stream[b] = x
        total = total + jnp.sum(x, axis=-1, keepdims=True)

    def over_parts(column):
        wide = jnp.broadcast_to(column, (window, 128))
        out = wide
        for j in range(1, parts):
            out = out + pltpu.roll(wide, j * owned, 0)
        return out[:, 0:1]

    full = pools * block
    mean = over_parts(total) * (1.0 / full)
    square = jnp.zeros((window, 1), jnp.float32)
    for b in range(pools):
        centre = stream[b] - mean
        square = square + jnp.sum(centre * centre, axis=-1, keepdims=True)
    inv_std = lax.rsqrt(over_parts(square) * (1.0 / full) + 1e-05)
    for b in range(pools):
        msg_b[b] = ((stream[b] - mean) * inv_std * gain_s[b]).astype(jnp.bfloat16)

    exchange(lambda to: msg_b.at[to % heads], land_b, b_s, b_r, 0)
    land_b[me] = msg_b[h]
    exchange(gate_src, gate_land, g_s, g_r, 1)
    for t in range(devices):
        gate_rows[t * owned : (t + 1) * owned, :] = gate_land[t, 0:owned, :]
    exchange(lambda to: msg_b.at[to % heads], land_b, b_s, b_r, 1)
    for t in range(devices):
        x = land_b[t].astype(jnp.float32)
        for j in range(parts):
            big[t * owned : (t + 1) * owned, j * piece : (j + 1) * piece] = x[
                j * owned : (j + 1) * owned
            ]
    rows = big[...].astype(jnp.bfloat16)

    lanes = lax.broadcasted_iota(jnp.int32, (all_rows, 128), 1)
    r_at = lax.broadcasted_iota(jnp.int32, (all_rows, all_rows), 0)
    c_at = lax.broadcasted_iota(jnp.int32, (all_rows, all_rows), 1)
    earlier = jnp.where((r_at // owned == c_at // owned) & (c_at < r_at), 1.0, 0.0)
    slots = devices * cap
    row_at = lax.broadcasted_iota(jnp.int32, (all_rows, slots), 0)
    slot_at = lax.broadcasted_iota(jnp.int32, (all_rows, slots), 1)
    for l in range(2):
        weight = jnp.sum(
            jnp.where(lanes == p * 2 + l, gate_rows[...], 0.0), axis=-1, keepdims=True
        )
        member = jnp.where(weight > 0.0, 1.0, 0.0)
        rank = dot(
            earlier.astype(jnp.bfloat16),
            jnp.broadcast_to(member, (all_rows, 128)).astype(jnp.bfloat16),
        )[:, 0:1]
        place = (slot_at - row_at // owned * cap).astype(jnp.float32)
        table = jnp.where((place == rank) & (member > 0.0), 1.0, 0.0)
        merge[l] = table * weight
        rows_bf[l] = lax.dot_general(
            table.astype(jnp.bfloat16),
            rows,
            (((0,), (0,)), ((), ())),
            preferred_element_type=jnp.float32,
        ).astype(jnp.bfloat16)

    def hop(source, land, send, recv, k, to):
        return pltpu.make_async_remote_copy(
            src_ref=source,
            dst_ref=land,
            send_sem=send.at[k],
            recv_sem=recv.at[k],
            device_id={"pool": p, "heads": to},
            device_id_type=MESH,
        )

    def hop_a(k):
        return hop(a_send.at[k], a_land.at[k], ha_s, ha_r, k, sibling)

    def hop_b(k):
        return hop(b_send.at[k], b_land.at[k], hb_s, hb_r, k, across)

    def hop_c(k):
        return hop(hid.at[k, core], hid.at[k, core], hc_s, hc_r, k, sibling)

    acc[...] = jnp.zeros_like(acc)

    @pl.loop(0, chunks + 3)
    def _(i):
        @pl.when((i >= 1) & (i < chunks + 1))
        def _():
            k = i - 1
            hop_a(k).wait_recv()
            b_send[k] = (own[k % 2] + a_land[k].astype(jnp.float32)).astype(jnp.bfloat16)
            hop_b(k).start()

        @pl.when(i < chunks)
        def _():
            wait(ein_copies(i))
            slot = ein_slot(i)
            a_send[i] = (
                dot(rows_bf[1 - core, :, :width], wts[slot, 1 - core, 0])
                + dot(rows_bf[1 - core, :, width:], wts[slot, 1 - core, 1])
            ).astype(jnp.bfloat16)
            hop_a(i).start()
            own[i % 2] = dot(rows_bf[core, :, :width], wts[slot, core, 0]) + dot(
                rows_bf[core, :, width:], wts[slot, core, 1]
            )

            @pl.when(i + 1 + ahead < chunks)
            def _():
                start(eout_copies(i + 1 + ahead))

        @pl.when((i >= 2) & (i < chunks + 2))
        def _():
            k = i - 2
            hop_b(k).wait_recv()
            pre = b_send[k].astype(jnp.float32) + b_land[k].astype(jnp.float32)
            hid[k, core] = (pre / (1.0 + jnp.exp(-pre))).astype(jnp.bfloat16)
            hop_c(k).start()

        @pl.when(i >= 3)
        def _():
            k = i - 3
            wait(eout_copies(k))
            slot = eout_slot(k)
            for a in range(2):
                acc[core, :, a * width : (a + 1) * width] += dot(hid[k, core], wts[slot, core, a])
            hop_c(k).wait_recv()
            for a in range(2):
                acc[1 - core, :, a * width : (a + 1) * width] += dot(
                    hid[k, 1 - core], wts[slot, 1 - core, a]
                )

    result = jnp.zeros((all_rows, block), jnp.float32)
    for l in range(2):
        result = result + jnp.dot(
            merge[l],
            acc[l],
            precision=lax.Precision.HIGHEST,
            preferred_element_type=jnp.float32,
        )
    big[...] = result
    pack_into(msg_c)
    exchange(lambda to: msg_c.at[to], land_c, c_s, c_r, 0)
    land_c[me] = msg_c[me]
    exchange(lambda to: msg_c.at[to], land_c, c_s, c_r, 1)
    for i in range(heads):
        x = stream[i]
        for b in range(pools):
            x = x + land_c[b * heads + i].astype(jnp.float32)
        for j in range(parts):
            at = (i * parts + j) * piece
            flat[:, at : at + piece] = x[j * owned : (j + 1) * owned]
    out_ref[...] = flat[...].astype(out_ref.dtype)

    exchange(gate_src, gate_land, g_s, g_r, 2)
    for d in range(1, pools):
        att_copy(d).wait_send()
    exchange(lambda to: msg_a.at[to], land_a, a_s, a_r, 2)
    exchange(lambda to: msg_b.at[to % heads], land_b, b_s, b_r, 2)
    exchange(lambda to: msg_c.at[to], land_c, c_s, c_r, 2)

    @pl.loop(0, chunks)
    def _(k):
        hop_a(k).wait_send()
        hop_b(k).wait_send()
        hop_c(k).wait_send()


def fused(queries, new_kv, cache_kv, cache_len, residual, out_weight, norm_gain, expert_ids, gate_raw, expert_in, expert_out):
    pools, heads = lax.axis_size("pool"), lax.axis_size("heads")
    owned, features = residual.shape
    local, depth, hidden = expert_in.shape
    devices = pools * heads
    width = out_weight.shape[1] // 2
    chunks = hidden // width
    slots = devices * CAP
    window = queries.shape[0]
    all_rows = devices * owned
    block = out_weight.shape[1]
    piece = block * owned // window
    bf, f32 = jnp.bfloat16, jnp.float32
    vmem = pl.BlockSpec(memory_space=pltpu.VMEM)
    hbm = pl.BlockSpec(memory_space=pl.ANY)
    smem = pl.BlockSpec(memory_space=pltpu.SMEM)
    dma = pltpu.SemaphoreType.DMA
    msgs = (devices, window, piece)
    return pl.pallas_call(
        functools.partial(fused_kernel, (pools, heads, owned, chunks, width, CAP)),
        out_shape=jax.ShapeDtypeStruct((owned, features), bf),
        in_specs=[vmem, vmem, hbm, smem, vmem, hbm, vmem, vmem, vmem, hbm, hbm],
        out_specs=vmem,
        scratch_shapes=[
            pltpu.VMEM(cache_kv.shape, bf),
            pltpu.VMEM((SLOTS, local, 2, width, width), bf),
            pltpu.VMEM((8, 128), f32),
            pltpu.VMEM((devices, 8, 128), f32),
            pltpu.VMEM((all_rows, 128), f32),
            pltpu.VMEM((pools, window, queries.shape[1]), bf),
            pltpu.VMEM((all_rows, block), f32),
            pltpu.VMEM(msgs, f32),
            pltpu.VMEM(msgs, bf),
            pltpu.VMEM(msgs, bf),
            pltpu.VMEM((pools, window, piece), f32),
            pltpu.VMEM((pools, window, piece), f32),
            pltpu.VMEM((heads, window, piece), bf),
            pltpu.VMEM(msgs, bf),
            pltpu.VMEM((local, slots, block), bf),
            pltpu.VMEM((local, all_rows, slots), f32),
            pltpu.VMEM((2, slots, width), f32),
            pltpu.VMEM((chunks, slots, width), bf),
            pltpu.VMEM((chunks, slots, width), bf),
            pltpu.VMEM((chunks, slots, width), bf),
            pltpu.VMEM((chunks, slots, width), bf),
            pltpu.VMEM((chunks, local, slots, width), bf),
            pltpu.VMEM((local, slots, block), f32),
            pltpu.VMEM(msgs, bf),
            pltpu.VMEM(msgs, bf),
            pltpu.VMEM((owned, features), f32),
            dma,
            dma((2, 2)),
            dma((chunks, 2)),
            dma((chunks, 2)),
            dma((devices,)),
            dma((devices,)),
            dma((pools,)),
            dma((pools,)),
            dma((devices,)),
            dma((devices,)),
            dma((devices,)),
            dma((devices,)),
            dma((devices,)),
            dma((devices,)),
            dma((chunks,)),
            dma((chunks,)),
            dma((chunks,)),
            dma((chunks,)),
            dma((chunks,)),
            dma((chunks,)),
        ],
        compiler_params=pltpu.CompilerParams(
            collective_id=0, has_side_effects=True, vmem_limit_bytes=VMEM_LIMIT
        ),
    )(queries, new_kv, cache_kv, cache_len, residual, out_weight, norm_gain.reshape(1, -1), expert_ids, gate_raw, expert_in, expert_out)


def one_kernel(mesh, *args):
    queries, residual, out_weight, expert_in = args[0], args[4], args[5], args[9]
    pools, heads = mesh.shape["pool"], mesh.shape["heads"]
    window, owned, block = queries.shape[0], residual.shape[0], out_weight.shape[1]
    local, depth, hidden = expert_in.shape
    return (
        pools == heads
        and heads == 4
        and local == 2
        and pools * local == EXPERTS
        and window == heads * owned
        and window % 16 == 0
        and depth == block
        and queries.shape[1] == block
        and block % (heads * 128) == 0
        and hidden % (block // 2) == 0
        and SLOTS // 2 < hidden // (block // 2) < SLOTS - 1
        and pools * heads * CAP % 16 == 0
    )


def solution(mesh):
    placed = (
        P(("groups", "pool"), "heads"),
        P(None, ("groups", "pool"), "heads"),
        P(None, ("groups", "pool"), "heads"),
        P(("groups", "pool")),
        P(("groups", "pool", "heads"), None),
        P("heads", "pool"),
        P(),
        P(("groups", "pool", "heads"), None),
        P(("groups", "pool", "heads"), None),
        P("pool", "heads", None),
        P("pool", None, "heads"),
    )
    def on_blocks(*args):
        if one_kernel(mesh, *args):
            return fused(*args)
        return on_device(*args)

    return jax.shard_map(
        on_blocks,
        mesh=mesh,
        in_specs=placed,
        out_specs=P(("groups", "pool", "heads"), None),
        check_vma=False,
    )
```

```python
import functools

import jax
import jax.numpy as jnp
import numpy as np
from jax import lax
from jax.experimental import pallas as pl
from jax.experimental.pallas import tpu as pltpu
from jax.sharding import PartitionSpec as P

QHEADS = 48
KVHEADS = 8
HEAD_DIM = 128
EXPERTS = 8
NGRAM = 4
CAP = 3


def row_ids_lower(count):
    row_ids = jnp.arange(count, dtype=jnp.int32)
    return row_ids[:, None] > row_ids[None, :]


def on_device(
    queries,
    new_kv,
    cache_kv,
    cache_len,
    residual,
    out_weight,
    norm_gain,
    expert_ids,
    gate_raw,
    expert_in,
    expert_out,
):
    pool_size = lax.axis_size("pool")
    heads_count = lax.axis_size("heads")
    window_rows = queries.shape[0]
    kv_local = cache_kv.shape[2] // HEAD_DIM
    group = QHEADS // KVHEADS
    width = residual.shape[1]
    local_q = queries.reshape(window_rows, kv_local, group, HEAD_DIM)
    cache_keys = cache_kv[0].reshape(-1, kv_local, HEAD_DIM)
    cache_vals = cache_kv[1].reshape(-1, kv_local, HEAD_DIM)
    window_keys = new_kv[0].reshape(window_rows, kv_local, HEAD_DIM)
    window_vals = new_kv[1].reshape(window_rows, kv_local, HEAD_DIM)
    score_scale = 1.0 / HEAD_DIM**0.5
    cache_score = (
        jnp.einsum("rkgd,tkd->kgrt", local_q, cache_keys, preferred_element_type=jnp.float32)
        * score_scale
    )
    window_score = (
        jnp.einsum("rkgd,skd->kgrs", local_q, window_keys, preferred_element_type=jnp.float32)
        * score_scale
    )
    positions = jnp.arange(cache_keys.shape[0], dtype=jnp.int32)
    cache_mask = (positions < cache_len[0])[None, None, None, :]
    row_ids = jnp.arange(window_rows, dtype=jnp.int32)
    same_gram = row_ids[:, None] // NGRAM == row_ids[None, :] // NGRAM
    window_mask = (same_gram & (row_ids[None, :] <= row_ids[:, None]))[None, None]
    cache_score = jnp.where(cache_mask, cache_score, -1e30)
    window_score = jnp.where(window_mask, window_score, -1e30)
    row_max = jnp.maximum(jnp.max(cache_score, axis=-1), jnp.max(window_score, axis=-1))[..., None]
    cache_exp = jnp.where(cache_mask, jnp.exp(cache_score - row_max), 0.0)
    window_exp = jnp.where(window_mask, jnp.exp(window_score - row_max), 0.0)
    denom = (jnp.sum(cache_exp, axis=-1) + jnp.sum(window_exp, axis=-1))[..., None]
    cache_prob = (cache_exp / denom).astype(jnp.bfloat16)
    window_prob = (window_exp / denom).astype(jnp.bfloat16)
    combined = jnp.einsum(
        "kgrt,tkd->rkgd", cache_prob, cache_vals, preferred_element_type=jnp.float32
    )
    combined = combined + jnp.einsum(
        "kgrs,skd->rkgd", window_prob, window_vals, preferred_element_type=jnp.float32
    )
    attended = combined.reshape(window_rows, -1).astype(jnp.bfloat16)
    partial_value = jnp.dot(
        lax.all_gather(attended, "pool", axis=0, tiled=True),
        out_weight,
        preferred_element_type=jnp.float32,
    )
    partial_value = partial_value.reshape(pool_size, window_rows, -1)
    summed = lax.psum_scatter(
        partial_value.astype(jnp.bfloat16), "heads", scatter_dimension=1, tiled=True
    ).astype(jnp.float32)
    projected = lax.all_to_all(
        summed.astype(jnp.bfloat16), "pool", split_axis=0, concat_axis=2, tiled=True
    ).astype(summed.dtype)[0]
    stream = residual.astype(jnp.float32) + projected
    centre = stream - jnp.mean(stream, axis=-1, keepdims=True)
    spread = jnp.mean(centre * centre, axis=-1, keepdims=True)
    normed = (centre * lax.rsqrt(spread + 1e-05) * norm_gain).astype(jnp.bfloat16)
    resident_rows = normed.shape[0]
    slices = max(pool_size // EXPERTS, 1)
    local_count = expert_in.shape[0]
    slot_count = CAP
    owner_index = np.arange(local_count * pool_size)
    owner_expert = (owner_index % pool_size * local_count + owner_index // pool_size) // slices
    expert_owner_lookup = jnp.asarray(
        (owner_expert[:, None] == np.arange(EXPERTS)[None, :]).astype(np.float32)
    )
    selected_experts = (expert_ids[:, :, None] == jnp.arange(EXPERTS, dtype=jnp.int32)).astype(
        jnp.float32
    )
    member = jnp.sum(selected_experts, axis=1)
    before = row_ids_lower(resident_rows).astype(jnp.float32)
    rank_rows = jnp.dot(
        before, member, precision=lax.Precision.HIGHEST, preferred_element_type=jnp.float32
    )
    slot_index = jnp.sum(selected_experts * rank_rows[:, None, :], axis=2)
    slot_onehot_mask = (slot_index[:, :, None] == jnp.arange(slot_count, dtype=jnp.float32)).astype(
        jnp.float32
    )
    expert_location = jnp.einsum("vyu,vyt->vut", selected_experts, slot_onehot_mask)
    dispatch_table = jnp.einsum("ydr,ad->ary", expert_location, expert_owner_lookup).astype(
        jnp.bfloat16
    )
    sending = jnp.einsum(
        "jci,id->jcd", dispatch_table, normed, preferred_element_type=jnp.float32
    ).astype(jnp.bfloat16)
    outgoing = sending.reshape(
        local_count, pool_size, slot_count, heads_count, width // heads_count
    )
    received = lax.all_to_all(
        lax.all_to_all(outgoing, "pool", split_axis=1, concat_axis=1, tiled=True),
        "heads",
        split_axis=3,
        concat_axis=3,
        tiled=True,
    )
    routed_rows = pool_size * slot_count * heads_count
    rows_in = received.reshape(local_count, routed_rows, width // heads_count)
    pre_part = jnp.einsum("lmf,lfn->lmn", rows_in, expert_in, preferred_element_type=jnp.float32)
    hidden_total = lax.psum(pre_part.astype(jnp.bfloat16), "heads").astype(jnp.float32)
    hidden = jax.nn.silu(hidden_total).astype(jnp.bfloat16)
    result = jnp.einsum("lmn,lnd->lmd", hidden, expert_out, preferred_element_type=jnp.float32)
    result = result.reshape(local_count, pool_size, slot_count, heads_count, -1)
    gate_fraction = gate_raw / jnp.sum(gate_raw, axis=-1, keepdims=True)
    gate_scaled_output = jnp.einsum(
        "qv,qvg,qvr->qgr", gate_fraction, selected_experts, slot_onehot_mask
    )
    returned = lax.all_to_all(
        lax.all_to_all(
            result.astype(jnp.bfloat16), "pool", split_axis=1, concat_axis=1, tiled=True
        ),
        "heads",
        split_axis=3,
        concat_axis=3,
        tiled=True,
    ).astype(result.dtype)
    returned_flat = returned.reshape(local_count * pool_size * slot_count, width)
    merge_weight_table = jnp.einsum("gbu,db->gdu", gate_scaled_output, expert_owner_lookup).reshape(
        resident_rows, -1
    )
    expert_sum = jnp.dot(
        merge_weight_table,
        returned_flat,
        precision=lax.Precision.HIGHEST,
        preferred_element_type=jnp.float32,
    )
    return (stream + expert_sum).astype(jnp.bfloat16)


MESH = pl.DeviceIdType.MESH
VMEM_LIMIT = 62 * 2**20
SLOTS = 11


def dot(lhs, rhs):
    return jnp.dot(lhs, rhs, preferred_element_type=jnp.float32)


def fused_kernel(
    sizes,
    q_ref,
    nkv_ref,
    cache_ref,
    len_ref,
    res_ref,
    ow_ref,
    gain_ref,
    ids_ref,
    raw_ref,
    ein_ref,
    eout_ref,
    out_ref,
    cache_v,
    wts,
    gate_tile,
    gate_land,
    gate_rows,
    att,
    big,
    packed,
    msg_a,
    land_a,
    msg_s,
    land_s,
    stream,
    gain_s,
    msg_b,
    land_b,
    rows_bf,
    merge,
    own,
    a_send,
    a_land,
    b_send,
    b_land,
    hid,
    acc,
    msg_c,
    land_c,
    flat,
    s_cache,
    s_ow,
    s_ein,
    s_eout,
    g_s,
    g_r,
    t_s,
    t_r,
    a_s,
    a_r,
    b_s,
    b_r,
    c_s,
    c_r,
    ha_s,
    ha_r,
    hb_s,
    hb_r,
    hc_s,
    hc_r,
):
    pools, heads, owned, chunks, width, cap = sizes
    devices = pools * heads
    window = q_ref.shape[0]
    all_rows = devices * owned
    parts = window // owned
    block = ow_ref.shape[1]
    piece = block // parts
    p = lax.axis_index("pool")
    h = lax.axis_index("heads")
    me = p * heads + h
    core = h % 2
    sibling = (h // 2) * 2 + (1 - core)
    across = (h + 2) % heads

    def dev(flat_id):
        return {"pool": flat_id // heads, "heads": flat_id % heads}

    cache_copy = pltpu.make_async_copy(cache_ref, cache_v, s_cache)
    cache_copy.start()

    def span(k):
        return pl.ds(pl.multiple_of(k * width, width), width)

    def ow_copies():
        return [
            pltpu.make_async_copy(
                ow_ref.at[span(a), span(b)], wts.at[0, a, b], s_ow.at[a, b]
            )
            for a in range(2)
            for b in range(2)
        ]

    def ein_slot(k):
        return (1 + k) % SLOTS

    def eout_slot(k):
        return (1 + chunks + k) % SLOTS

    def ein_copies(k):
        return [
            pltpu.make_async_copy(
                ein_ref.at[:, span(a), span(k)], wts.at[ein_slot(k), :, a], s_ein.at[k, a]
            )
            for a in range(2)
        ]

    def eout_copies(k):
        return [
            pltpu.make_async_copy(
                eout_ref.at[:, span(k), span(a)], wts.at[eout_slot(k), :, a], s_eout.at[k, a]
            )
            for a in range(2)
        ]

    def start(copies):
        for copy in copies:
            copy.start()

    def wait(copies):
        for copy in copies:
            copy.wait()

    ahead = SLOTS - 1 - chunks
    start(ow_copies())

    barrier = pltpu.get_barrier_semaphore()

    @pl.loop(1, devices)
    def _(d):
        pl.semaphore_signal(
            barrier, inc=1, device_id=dev((me + d) % devices), device_id_type=MESH
        )

    pl.semaphore_wait(barrier, devices - 1)

    def exchange(source, land, send, recv, step):
        @pl.loop(1, devices)
        def _(d):
            to = (me + d) % devices
            copy = pltpu.make_async_remote_copy(
                src_ref=source(to),
                dst_ref=land.at[me],
                send_sem=send.at[d],
                recv_sem=recv.at[d],
                device_id=dev(to),
                device_id_type=MESH,
            )
            if step == 0:
                copy.start()
            elif step == 1:
                copy.wait_recv()
            else:
                copy.wait_send()

    ids = ids_ref[...]
    raw = raw_ref[...]
    share = raw / jnp.sum(raw, axis=-1, keepdims=True)
    lane = lax.broadcasted_iota(jnp.int32, (owned, 128), 1)
    table = jnp.zeros((owned, 128), jnp.float32)
    for v in range(ids_ref.shape[1]):
        table = table + jnp.where(lane == ids[:, v : v + 1], share[:, v : v + 1], 0.0)
    gate_tile[...] = jnp.zeros_like(gate_tile)
    gate_tile[0:owned, :] = table

    def gate_src(to):
        return gate_tile

    exchange(gate_src, gate_land, g_s, g_r, 0)
    gate_land[me] = gate_tile[...]

    residual = res_ref[...].astype(jnp.float32)
    for b in range(pools):
        for j in range(parts):
            at = (b * parts + j) * piece
            rows = slice(j * owned, (j + 1) * owned)
            stream[b, rows, :] = residual[:, at : at + piece]
            gain_s[b, rows, :] = jnp.broadcast_to(gain_ref[:, at : at + piece], (owned, piece))

    cache_copy.wait()
    for k in range(chunks):
        start(ein_copies(k))
    for k in range(ahead):
        start(eout_copies(k))
    kv_local = cache_ref.shape[2] // HEAD_DIM
    group = q_ref.shape[1] // HEAD_DIM // kv_local
    cached = cache_ref.shape[1]
    scale = 1.0 / HEAD_DIM**0.5
    length = len_ref[0]
    stacked = group * window
    cache_mask = lax.broadcasted_iota(jnp.int32, (stacked, cached), 1) < length
    row = lax.broadcasted_iota(jnp.int32, (stacked, window), 0) % window
    col = lax.broadcasted_iota(jnp.int32, (stacked, window), 1)
    window_mask = (row // NGRAM == col // NGRAM) & (col <= row)
    contract = (((1,), (1,)), ((), ()))
    for k in range(kv_local):
        at = slice(k * HEAD_DIM, (k + 1) * HEAD_DIM)
        q = jnp.concatenate(
            [
                q_ref[:, (k * group + g) * HEAD_DIM : (k * group + g + 1) * HEAD_DIM]
                for g in range(group)
            ],
            axis=0,
        )
        s_c = lax.dot_general(q, cache_v[0, :, at], contract, preferred_element_type=jnp.float32)
        s_w = lax.dot_general(q, nkv_ref[0, :, at], contract, preferred_element_type=jnp.float32)
        s_c = jnp.where(cache_mask, s_c * scale, -1e30)
        s_w = jnp.where(window_mask, s_w * scale, -1e30)
        top = jnp.maximum(
            jnp.max(s_c, axis=-1, keepdims=True), jnp.max(s_w, axis=-1, keepdims=True)
        )
        e_c = jnp.where(cache_mask, jnp.exp(s_c - top), 0.0)
        e_w = jnp.where(window_mask, jnp.exp(s_w - top), 0.0)
        inv = 1.0 / (
            jnp.sum(e_c, axis=-1, keepdims=True) + jnp.sum(e_w, axis=-1, keepdims=True)
        )
        o = dot((e_c * inv).astype(jnp.bfloat16), cache_v[1, :, at])
        o = o + dot((e_w * inv).astype(jnp.bfloat16), nkv_ref[1, :, at])
        o = o.astype(jnp.bfloat16)
        for g in range(group):
            att[p, :, (k * group + g) * HEAD_DIM : (k * group + g + 1) * HEAD_DIM] = o[
                g * window : (g + 1) * window
            ]

    def att_copy(d):
        return pltpu.make_async_remote_copy(
            src_ref=att.at[p],
            dst_ref=att.at[p],
            send_sem=t_s.at[d],
            recv_sem=t_r.at[d],
            device_id={"pool": (p + d) % pools, "heads": h},
            device_id_type=MESH,
        )

    for d in range(1, pools):
        att_copy(d).start()
    for d in range(1, pools):
        att_copy(d).wait_recv()
    wait(ow_copies())
    gathered = jnp.concatenate([att[b] for b in range(pools)], axis=0)
    for b in range(2):
        big[:, b * width : (b + 1) * width] = dot(gathered[:, :width], wts[0, 0, b]) + dot(
            gathered[:, width:], wts[0, 1, b]
        )
    start(eout_copies(ahead))

    def pack_into(msg):
        for t in range(devices):
            for j in range(parts):
                packed[t, j * owned : (j + 1) * owned, :] = big[
                    t * owned : (t + 1) * owned, j * piece : (j + 1) * piece
                ]
        msg[...] = packed[...].astype(jnp.bfloat16)

    pack_into(msg_a)

    def to_heads(d, b):
        to = (h + d) % heads
        return pltpu.make_async_remote_copy(
            src_ref=msg_a.at[b * heads + to],
            dst_ref=land_a.at[h * pools + b],
            send_sem=a_s.at[d * pools + b],
            recv_sem=a_r.at[d * pools + b],
            device_id={"pool": p, "heads": to},
            device_id_type=MESH,
        )

    def to_pool(d):
        to = (p + d) % pools
        return pltpu.make_async_remote_copy(
            src_ref=msg_s.at[to],
            dst_ref=land_s.at[p],
            send_sem=a_s.at[d],
            recv_sem=a_r.at[d],
            device_id={"pool": to, "heads": h},
            device_id_type=MESH,
        )

    pairs = [(d, b) for d in range(1, heads) for b in range(pools)]
    for d, b in pairs:
        to_heads(d, b).start()
    for b in range(pools):
        land_a[h * pools + b] = msg_a[b * heads + h]
    for d, b in pairs:
        to_heads(d, b).wait_recv()
    for b in range(pools):
        x = land_a[b].astype(jnp.float32)
        for i in range(1, heads):
            x = x + land_a[i * pools + b].astype(jnp.float32)
        msg_s[b] = x.astype(jnp.bfloat16)
    for d in range(1, pools):
        to_pool(d).start()
    land_s[p] = msg_s[p]
    for d in range(1, pools):
        to_pool(d).wait_recv()

    total = jnp.zeros((window, 1), jnp.float32)
    for b in range(pools):
        x = stream[b] + land_s[b].astype(jnp.float32)
        stream[b] = x
        total = total + jnp.sum(x, axis=-1, keepdims=True)

    def over_parts(column):
        wide = jnp.broadcast_to(column, (window, 128))
        out = wide
        for j in range(1, parts):
            out = out + pltpu.roll(wide, j * owned, 0)
        return out[:, 0:1]

    full = pools * block
    mean = over_parts(total) * (1.0 / full)
    square = jnp.zeros((window, 1), jnp.float32)
    for b in range(pools):
        centre = stream[b] - mean
        square = square + jnp.sum(centre * centre, axis=-1, keepdims=True)
    inv_std = lax.rsqrt(over_parts(square) * (1.0 / full) + 1e-05)
    for b in range(pools):
        msg_b[b] = ((stream[b] - mean) * inv_std * gain_s[b]).astype(jnp.bfloat16)

    exchange(lambda to: msg_b.at[to % heads], land_b, b_s, b_r, 0)
    land_b[me] = msg_b[h]
    exchange(gate_src, gate_land, g_s, g_r, 1)
    for t in range(devices):
        gate_rows[t * owned : (t + 1) * owned, :] = gate_land[t, 0:owned, :]
    exchange(lambda to: msg_b.at[to % heads], land_b, b_s, b_r, 1)
    for t in range(devices):
        x = land_b[t].astype(jnp.float32)
        for j in range(parts):
            big[t * owned : (t + 1) * owned, j * piece : (j + 1) * piece] = x[
                j * owned : (j + 1) * owned
            ]
    rows = big[...].astype(jnp.bfloat16)

    lanes = lax.broadcasted_iota(jnp.int32, (all_rows, 128), 1)
    r_at = lax.broadcasted_iota(jnp.int32, (all_rows, all_rows), 0)
    c_at = lax.broadcasted_iota(jnp.int32, (all_rows, all_rows), 1)
    earlier = jnp.where((r_at // owned == c_at // owned) & (c_at < r_at), 1.0, 0.0)
    slots = devices * cap
    row_at = lax.broadcasted_iota(jnp.int32, (all_rows, slots), 0)
    slot_at = lax.broadcasted_iota(jnp.int32, (all_rows, slots), 1)
    for l in range(2):
        weight = jnp.sum(
            jnp.where(lanes == p * 2 + l, gate_rows[...], 0.0), axis=-1, keepdims=True
        )
        member = jnp.where(weight > 0.0, 1.0, 0.0)
        rank = dot(
            earlier.astype(jnp.bfloat16),
            jnp.broadcast_to(member, (all_rows, 128)).astype(jnp.bfloat16),
        )[:, 0:1]
        place = (slot_at - row_at // owned * cap).astype(jnp.float32)
        table = jnp.where((place == rank) & (member > 0.0), 1.0, 0.0)
        merge[l] = table * weight
        rows_bf[l] = lax.dot_general(
            table.astype(jnp.bfloat16),
            rows,
            (((0,), (0,)), ((), ())),
            preferred_element_type=jnp.float32,
        ).astype(jnp.bfloat16)

    def hop(source, land, send, recv, k, to):
        return pltpu.make_async_remote_copy(
            src_ref=source,
            dst_ref=land,
            send_sem=send.at[k],
            recv_sem=recv.at[k],
            device_id={"pool": p, "heads": to},
            device_id_type=MESH,
        )

    def hop_a(k):
        return hop(a_send.at[k], a_land.at[k], ha_s, ha_r, k, sibling)

    def hop_b(k):
        return hop(b_send.at[k], b_land.at[k], hb_s, hb_r, k, across)

    def hop_c(k):
        return hop(hid.at[k, core], hid.at[k, core], hc_s, hc_r, k, sibling)

    acc[...] = jnp.zeros_like(acc)

    @pl.loop(0, chunks + 3)
    def _(i):
        @pl.when((i >= 1) & (i < chunks + 1))
        def _():
            k = i - 1
            hop_a(k).wait_recv()
            b_send[k] = (own[k % 2] + a_land[k].astype(jnp.float32)).astype(jnp.bfloat16)
            hop_b(k).start()

        @pl.when(i < chunks)
        def _():
            wait(ein_copies(i))
            slot = ein_slot(i)
            a_send[i] = (
                dot(rows_bf[1 - core, :, :width], wts[slot, 1 - core, 0])
                + dot(rows_bf[1 - core, :, width:], wts[slot, 1 - core, 1])
            ).astype(jnp.bfloat16)
            hop_a(i).start()
            own[i % 2] = dot(rows_bf[core, :, :width], wts[slot, core, 0]) + dot(
                rows_bf[core, :, width:], wts[slot, core, 1]
            )

            @pl.when(i + 1 + ahead < chunks)
            def _():
                start(eout_copies(i + 1 + ahead))

        @pl.when((i >= 2) & (i < chunks + 2))
        def _():
            k = i - 2
            hop_b(k).wait_recv()
            pre = b_send[k].astype(jnp.float32) + b_land[k].astype(jnp.float32)
            hid[k, core] = (pre / (1.0 + jnp.exp(-pre))).astype(jnp.bfloat16)
            hop_c(k).start()

        @pl.when(i >= 3)
        def _():
            k = i - 3
            wait(eout_copies(k))
            slot = eout_slot(k)
            for a in range(2):
                acc[core, :, a * width : (a + 1) * width] += dot(hid[k, core], wts[slot, core, a])
            hop_c(k).wait_recv()
            for a in range(2):
                acc[1 - core, :, a * width : (a + 1) * width] += dot(
                    hid[k, 1 - core], wts[slot, 1 - core, a]
                )

    result = jnp.zeros((all_rows, block), jnp.float32)
    for l in range(2):
        result = result + jnp.dot(
            merge[l],
            acc[l],
            precision=lax.Precision.HIGHEST,
            preferred_element_type=jnp.float32,
        )
    big[...] = result
    pack_into(msg_c)
    exchange(lambda to: msg_c.at[to], land_c, c_s, c_r, 0)
    land_c[me] = msg_c[me]
    exchange(lambda to: msg_c.at[to], land_c, c_s, c_r, 1)
    for i in range(heads):
        x = stream[i]
        for b in range(pools):
            x = x + land_c[b * heads + i].astype(jnp.float32)
        for j in range(parts):
            at = (i * parts + j) * piece
            flat[:, at : at + piece] = x[j * owned : (j + 1) * owned]
    out_ref[...] = flat[...].astype(out_ref.dtype)

    exchange(gate_src, gate_land, g_s, g_r, 2)
    for d in range(1, pools):
        att_copy(d).wait_send()
    for d, b in pairs:
        to_heads(d, b).wait_send()
    for d in range(1, pools):
        to_pool(d).wait_send()
    exchange(lambda to: msg_b.at[to % heads], land_b, b_s, b_r, 2)
    exchange(lambda to: msg_c.at[to], land_c, c_s, c_r, 2)

    @pl.loop(0, chunks)
    def _(k):
        hop_a(k).wait_send()
        hop_b(k).wait_send()
        hop_c(k).wait_send()


def fused(queries, new_kv, cache_kv, cache_len, residual, out_weight, norm_gain, expert_ids, gate_raw, expert_in, expert_out):
    pools, heads = lax.axis_size("pool"), lax.axis_size("heads")
    owned, features = residual.shape
    local, depth, hidden = expert_in.shape
    devices = pools * heads
    width = out_weight.shape[1] // 2
    chunks = hidden // width
    slots = devices * CAP
    window = queries.shape[0]
    all_rows = devices * owned
    block = out_weight.shape[1]
    piece = block * owned // window
    bf, f32 = jnp.bfloat16, jnp.float32
    vmem = pl.BlockSpec(memory_space=pltpu.VMEM)
    hbm = pl.BlockSpec(memory_space=pl.ANY)
    smem = pl.BlockSpec(memory_space=pltpu.SMEM)
    dma = pltpu.SemaphoreType.DMA
    msgs = (devices, window, piece)
    return pl.pallas_call(
        functools.partial(fused_kernel, (pools, heads, owned, chunks, width, CAP)),
        out_shape=jax.ShapeDtypeStruct((owned, features), bf),
        in_specs=[vmem, vmem, hbm, smem, vmem, hbm, vmem, vmem, vmem, hbm, hbm],
        out_specs=vmem,
        scratch_shapes=[
            pltpu.VMEM(cache_kv.shape, bf),
            pltpu.VMEM((SLOTS, local, 2, width, width), bf),
            pltpu.VMEM((8, 128), f32),
            pltpu.VMEM((devices, 8, 128), f32),
            pltpu.VMEM((all_rows, 128), f32),
            pltpu.VMEM((pools, window, queries.shape[1]), bf),
            pltpu.VMEM((all_rows, block), f32),
            pltpu.VMEM(msgs, f32),
            pltpu.VMEM(msgs, bf),
            pltpu.VMEM(msgs, bf),
            pltpu.VMEM((pools, window, piece), bf),
            pltpu.VMEM((pools, window, piece), bf),
            pltpu.VMEM((pools, window, piece), f32),
            pltpu.VMEM((pools, window, piece), f32),
            pltpu.VMEM((heads, window, piece), bf),
            pltpu.VMEM(msgs, bf),
            pltpu.VMEM((local, slots, block), bf),
            pltpu.VMEM((local, all_rows, slots), f32),
            pltpu.VMEM((2, slots, width), f32),
            pltpu.VMEM((chunks, slots, width), bf),
            pltpu.VMEM((chunks, slots, width), bf),
            pltpu.VMEM((chunks, slots, width), bf),
            pltpu.VMEM((chunks, slots, width), bf),
            pltpu.VMEM((chunks, local, slots, width), bf),
            pltpu.VMEM((local, slots, block), f32),
            pltpu.VMEM(msgs, bf),
            pltpu.VMEM(msgs, bf),
            pltpu.VMEM((owned, features), f32),
            dma,
            dma((2, 2)),
            dma((chunks, 2)),
            dma((chunks, 2)),
            dma((devices,)),
            dma((devices,)),
            dma((pools,)),
            dma((pools,)),
            dma((devices,)),
            dma((devices,)),
            dma((devices,)),
            dma((devices,)),
            dma((devices,)),
            dma((devices,)),
            dma((chunks,)),
            dma((chunks,)),
            dma((chunks,)),
            dma((chunks,)),
            dma((chunks,)),
            dma((chunks,)),
        ],
        compiler_params=pltpu.CompilerParams(
            collective_id=0, has_side_effects=True, vmem_limit_bytes=VMEM_LIMIT
        ),
    )(queries, new_kv, cache_kv, cache_len, residual, out_weight, norm_gain.reshape(1, -1), expert_ids, gate_raw, expert_in, expert_out)


def one_kernel(mesh, *args):
    queries, residual, out_weight, expert_in = args[0], args[4], args[5], args[9]
    pools, heads = mesh.shape["pool"], mesh.shape["heads"]
    window, owned, block = queries.shape[0], residual.shape[0], out_weight.shape[1]
    local, depth, hidden = expert_in.shape
    return (
        pools == heads
        and heads == 4
        and local == 2
        and pools * local == EXPERTS
        and window == heads * owned
        and window % 16 == 0
        and depth == block
        and queries.shape[1] == block
        and block % (heads * 128) == 0
        and hidden % (block // 2) == 0
        and SLOTS // 2 < hidden // (block // 2) < SLOTS - 1
        and pools * heads * CAP % 16 == 0
    )


def solution(mesh):
    placed = (
        P(("groups", "pool"), "heads"),
        P(None, ("groups", "pool"), "heads"),
        P(None, ("groups", "pool"), "heads"),
        P(("groups", "pool")),
        P(("groups", "pool", "heads"), None),
        P("heads", "pool"),
        P(),
        P(("groups", "pool", "heads"), None),
        P(("groups", "pool", "heads"), None),
        P("pool", "heads", None),
        P("pool", None, "heads"),
    )
    def on_blocks(*args):
        if one_kernel(mesh, *args):
            return fused(*args)
        return on_device(*args)

    return jax.shard_map(
        on_blocks,
        mesh=mesh,
        in_specs=placed,
        out_specs=P(("groups", "pool", "heads"), None),
        check_vma=False,
    )
```
